256 devices in a mesh: outer: 8 (over x, core), inner: 32 (over z, y).
Axes of the slice: x: 4, y: 4, z: 8, core: 2. Of those that a mesh axis runs over, the one named last changes fastest.
Arguments:
- query_rows: bfloat16 [98304, 2048], P(('outer', 'inner')), may hold values from -1.5 to 1.5
- key_rows: bfloat16 [98304, 2048], P(('outer', 'inner')), may hold values from -6 to 6
- value_rows: bfloat16 [98304, 2048], P(('outer', 'inner')), may hold values from -6 to 6
- grad_output: bfloat16 [98304, 2048], P(('outer', 'inner')), may hold values from -0.59765625 to 0.59765625
Outputs:
- grad_query: bfloat16 [98304, 2048], P(('outer', 'inner'))
- grad_key: bfloat16 [98304, 2048], P(('outer', 'inner'))
- grad_value: bfloat16 [98304, 2048], P(('outer', 'inner'))
The draws below stay inside these ranges and needn't reach their ends.
All inputs are finite; a program needn't handle non-finite values.
Results may differ from the reference program's by a relative error of at most 0.0058.
Values may be sent and summed in bfloat16 or wider, within the bound.
A program may use at most 64 MiB of HBM per device.

```python
import jax
import jax.numpy as jnp
from jax import lax

HEADS = 16
HEAD = 128
TOK_DEV = 384
TOKENS = 98304


def block_levels(own_key, extent, pieces, smallest, largest):
    loudness = 1.0
    for dim, blocks in pieces:
        steps = jax.random.uniform(jax.random.fold_in(jax.random.fold_in(own_key, 6), dim), (blocks,), jnp.float32, smallest / len(pieces), largest / len(pieces))
        loudness = loudness * jnp.repeat(jnp.exp(steps), extent[dim] // blocks).reshape((-1,) + (1,) * (len(extent) - 1 - dim))
    return loudness


def normal_values(rng, shape, scale, most, cuts=(), kind=jnp.bfloat16):
    values = jax.random.normal(rng, shape, jnp.float32) * scale
    if len(cuts) > 0:
        values = block_levels(rng, shape, cuts, -0.22, 0.18) * values
    return jnp.clip(values, min=-most, max=most).astype(kind)


def setup_inputs(seed: int = 0) -> dict:
    streams_of = jax.random.split(jax.random.key(seed), 5)
    query_rows = normal_values(streams_of[0], (TOKENS, HEADS * HEAD), 0.25, 1.5, ((0, 256),))
    key_rows = normal_values(streams_of[1], (TOKENS, HEADS * HEAD), 1.0, 6.0, ((0, 256),))
    value_rows = normal_values(streams_of[2], (TOKENS, HEADS * HEAD), 1.0, 6.0, ((0, 256),))
    grad_output = normal_values(streams_of[3], (TOKENS, HEADS * HEAD), 0.1, 0.59765625, ((0, 256),))
    return {"query_rows": query_rows, "key_rows": key_rows, "value_rows": value_rows, "grad_output": grad_output}


def block_grads(query, key, value, grad, scales, prefix, suffix):
    query = query.astype(jnp.float32)
    key = key.astype(jnp.float32)
    value = value.astype(jnp.float32)
    grad = grad.astype(jnp.float32)
    order = lax.iota(jnp.int32, query.shape[0])
    causal = (order[None, :] <= order[:, None])[None]
    prod_out = jnp.einsum('the,she->hts', grad, value)
    prod_in = jnp.einsum('thd,shd->hts', query, key)
    weight_out = (jnp.where(causal, prod_out, 0.0) * scales[None, :, None]).astype(jnp.bfloat16).astype(jnp.float32)
    weight_in = (jnp.where(causal, prod_in, 0.0) * scales[None, :, None]).astype(jnp.bfloat16).astype(jnp.float32)
    prefix = prefix.astype(jnp.float32)
    suffix = suffix.astype(jnp.float32)
    grad_q = scales[:, None, None] * jnp.einsum('the,hde->thd', grad, prefix) + jnp.einsum('hts,shd->thd', weight_out, key)
    grad_k = jnp.einsum('she,hde->shd', value, suffix) + jnp.einsum('hts,thd->shd', weight_out, query)
    grad_v = jnp.einsum('shd,hde->she', key, suffix) + jnp.einsum('hts,the->she', weight_in, grad)
    return (grad_q.astype(jnp.bfloat16), grad_k.astype(jnp.bfloat16), grad_v.astype(jnp.bfloat16))

def reference(query_rows, key_rows, value_rows, grad_output):
    count = TOKENS // TOK_DEV

    def split(array):
        return array.reshape(count, TOK_DEV, HEADS, HEAD)
    positions = jnp.arange(TOKENS, dtype=jnp.float32).reshape(count, TOK_DEV)
    scales = 1.0 / jnp.sqrt(positions + 1.0)

    def forward(state, blocks):
        key, value = blocks
        update = jnp.einsum('shd,she->hde', key.astype(jnp.float32), value.astype(jnp.float32))
        return (state + update, state.astype(jnp.bfloat16))

    def backward(state, blocks):
        query, grad, block_scales = blocks
        scaled = (grad.astype(jnp.float32) * block_scales[:, None, None]).astype(jnp.bfloat16)
        update = jnp.einsum('thd,the->hde', query.astype(jnp.float32), scaled.astype(jnp.float32))
        return (state + update, state.astype(jnp.bfloat16))
    start = jnp.zeros((HEADS, HEAD, HEAD), jnp.float32)
    _, prefix_states = lax.scan(forward, start, (split(key_rows), split(value_rows)))
    _, suffix_states = lax.scan(backward, start, (split(query_rows), split(grad_output), scales), reverse=True)

    def one_block(blocks):
        return block_grads(*blocks)
    grad_q, grad_k, grad_v = lax.map(one_block, (split(query_rows), split(key_rows), split(value_rows), split(grad_output), scales, prefix_states, suffix_states))
    width = HEADS * HEAD
    return (grad_q.reshape(TOKENS, width), grad_k.reshape(TOKENS, width), grad_v.reshape(TOKENS, width))
```

```python
import functools

import jax
import jax.numpy as jnp
from jax import lax
from jax.experimental import pallas as pl
from jax.experimental.pallas import tpu as pltpu
from jax.sharding import PartitionSpec as P

MESH = pl.DeviceIdType.MESH
HEADS = 16
HEAD = 128
NY = 4
CHUNKS = 4
F32 = jnp.float32
BF16 = jnp.bfloat16

NN = (((1,), (0,)), ((), ()))
NT = (((1,), (1,)), ((), ()))
TN = (((0,), (0,)), ((), ()))


def dot(a, b, dims):
    return lax.dot_general(a, b, dims, preferred_element_type=F32)


def far_first(count):
    return sorted(range(1, count), key=lambda step: -min(step, count - step))


def schedule():
    order = []
    for c in range(CHUNKS):
        order.append(("S", c))
    order.append(("I", 0, 6))
    order.append(("R", 0))
    order.append(("I", 6, 8))
    order.append(("R", 1))
    order.append(("I", 8, 10))
    order.append(("R", 2))
    order.append(("T", 0))
    order.append(("I", 10, 12))
    order.append(("R", 3))
    order.append(("T", 1))
    order.append(("Z", 0))
    order.append(("I", 12, 14))
    order.append(("T", 2))
    order.append(("Z", 1))
    order.append(("I", 14, 16))
    order.append(("T", 3))
    order.append(("P", 0))
    order.append(("Z", 2))
    order.append(("P", 1))
    order.append(("Z", 3))
    order.append(("P", 2))
    order.append(("F", 0))
    order.append(("P", 3))
    order.append(("F", 1))
    order.append(("F", 2))
    order.append(("F", 3))
    return order


def kernel(
    no, nz,
    q_hbm, k_hbm, v_hbm, g_hbm,
    oq_hbm, ok_hbm, ov_hbm,
    q, k, v, g, sg, pq, pk, pv, oq, ok, ov,
    ysend, yrecv, zsend, zrecv, tsend, trecv, bsend, brecv, psend, precv,
    in_sem, out_sem, send_sem, recv_sem,
):
    length = q.shape[0]
    per = HEADS // CHUNKS
    width = per * HEAD
    sub = HEAD // nz
    o = lax.axis_index("outer")
    i = lax.axis_index("inner")
    z = i // NY
    y = i % NY

    ypeers = [lax.rem(y + d, NY) for d in far_first(NY)]
    zpeers = [lax.rem(z + d, nz) for d in far_first(nz)]
    opeers = [lax.rem(o + d, no) for d in far_first(no)]

    def loads(c):
        cols = pl.ds(c * width, width)
        return [
            pltpu.make_async_copy(src.at[:, cols], dst.at[:, cols], in_sem.at[c, j])
            for j, (src, dst) in enumerate(((k_hbm, k), (v_hbm, v), (g_hbm, g), (q_hbm, q)))
        ]

    for c in range(CHUNKS):
        for copy in loads(c):
            copy.start()

    barrier = pltpu.get_barrier_semaphore()
    everyone = (
        [(o, z * NY + p) for p in ypeers]
        + [(o, p * NY + y) for p in zpeers]
        + [(p, i) for p in opeers]
    )
    for peer in everyone:
        pl.semaphore_signal(barrier, inc=1, device_id=peer, device_id_type=MESH)

    offset = (o * (nz * NY) + i) * length
    rows = lax.broadcasted_iota(jnp.int32, (length, HEAD), 0) + offset
    scales = lax.rsqrt(rows.astype(F32) + 1.0)

    def send(src, dst, stage, c, peer):
        pltpu.make_async_remote_copy(
            src_ref=src, dst_ref=dst, send_sem=send_sem.at[stage], recv_sem=recv_sem.at[stage, c],
            device_id=peer, device_id_type=MESH,
        ).start()

    def arrived(ref, stage, c):
        pltpu.make_async_copy(ref, ref, recv_sem.at[stage, c]).wait()

    def states(c):
        for copy in loads(c):
            copy.wait()
        for j in range(per):
            cols = pl.ds((c * per + j) * HEAD, HEAD)
            ysend[c * NY + j, 0] = dot(k[:, cols], v[:, cols], TN).astype(BF16)
            scaled = (g[:, cols].astype(F32) * scales).astype(BF16)
            sg[:, cols] = scaled
            ysend[c * NY + j, 1] = dot(q[:, cols], scaled, TN).astype(BF16)
        if c == 0:
            pl.semaphore_wait(barrier, len(everyone))
        for p in ypeers:
            send(ysend.at[c * NY + p], yrecv.at[c, y], 0, c, (o, z * NY + p))
        yrecv[c, y] = ysend[c * NY + y]

    def group_sums(c):
        arrived(yrecv.at[c, pl.ds(0, NY - 1)], 0, c)
        total = yrecv[c, 0].astype(F32)
        for p in range(1, NY):
            total = total + yrecv[c, p].astype(F32)
        total = total.astype(BF16)
        for p in range(nz):
            zsend[c * nz + p] = total[:, p * sub:(p + 1) * sub, :]
        for p in zpeers:
            send(zsend.at[c * nz + p], zrecv.at[c, z], 1, c, (o, p * NY + y))
        zrecv[c, z] = zsend[c * nz + z]

    def outer_totals(c):
        arrived(zrecv.at[c, pl.ds(0, nz - 1)], 1, c)
        tsend[c] = jnp.sum(zrecv[c].astype(F32), axis=0)
        for p in opeers:
            kind = jnp.where(p > o, 0, 1)
            send(tsend.at[c, kind], trecv.at[c, o], 2, c, (p, i))
        trecv[c, o] = jnp.zeros((sub, HEAD), F32)

    def offsets(c):
        arrived(trecv.at[c, pl.ds(0, no - 1)], 2, c)
        before = jnp.zeros((sub, HEAD), F32)
        after = jnp.zeros((sub, HEAD), F32)
        for p in range(no):
            part = trecv[c, p]
            before = before + jnp.where(p < o, part, 0.0)
            after = after + jnp.where(p > o, part, 0.0)
        for p in range(nz):
            bsend[c * nz + p, 0] = before.astype(BF16)
            before = before + zrecv[c, p, 0].astype(F32)
        for p in reversed(range(nz)):
            bsend[c * nz + p, 1] = after.astype(BF16)
            after = after + zrecv[c, p, 1].astype(F32)
        for p in zpeers:
            send(bsend.at[c * nz + p], brecv.at[c, z], 3, c, (o, p * NY + y))
        brecv[c, z] = bsend[c * nz + z]

    def block_states(c):
        arrived(brecv.at[c, pl.ds(0, nz - 1)], 3, c)
        for p in range(nz):
            part = pl.ds(p * sub, sub)
            before = brecv[c, p, 0].astype(F32)
            for r in range(NY):
                psend[c * NY + r, 0, part] = before.astype(BF16)
                before = before + yrecv[c, r, 0, part].astype(F32)
            after = brecv[c, p, 1].astype(F32)
            for r in reversed(range(NY)):
                psend[c * NY + r, 1, part] = after.astype(BF16)
                after = after + yrecv[c, r, 1, part].astype(F32)
        for p in ypeers:
            send(psend.at[c * NY + p], precv.at[c, y], 4, c, (o, z * NY + p))
        precv[c, y] = psend[c * NY + y]

    def stores(c):
        cols = pl.ds(c * width, width)
        return [
            pltpu.make_async_copy(src.at[:, cols], dst.at[:, cols], out_sem.at[c, j])
            for j, (src, dst) in enumerate(((oq, oq_hbm), (ok, ok_hbm), (ov, ov_hbm)))
        ]

    def finish(c):
        arrived(precv.at[c, pl.ds(0, NY - 1)], 4, c)
        for j in range(per):
            cols = pl.ds((c * per + j) * HEAD, HEAD)
            prefix = precv[c, j, 0]
            suffix = precv[c, j, 1]
            oq[:, cols] = (pq[:, cols] + dot(sg[:, cols], prefix, NT)).astype(BF16)
            ok[:, cols] = (pk[:, cols] + dot(v[:, cols], suffix, NT)).astype(BF16)
            ov[:, cols] = (pv[:, cols] + dot(k[:, cols], suffix, NN)).astype(BF16)
        for copy in stores(c):
            copy.start()

    cut = length - HEAD

    def inside(head, carry):
        cols = pl.ds(pl.multiple_of(head * HEAD, HEAD), HEAD)
        kh, vh, qh, sh = k[:, cols], v[:, cols], q[:, cols], sg[:, cols]
        first = lax.broadcasted_iota(jnp.int32, (length, cut), 0)
        second = lax.broadcasted_iota(jnp.int32, (length, cut), 1)
        lower = second <= first
        upper = first <= second + HEAD
        row = lax.broadcasted_iota(jnp.int32, (HEAD, HEAD), 0)
        col = lax.broadcasted_iota(jnp.int32, (HEAD, HEAD), 1)

        def masked(a, b, mask):
            return jnp.where(mask, dot(a, b, NT), 0.0).astype(BF16)

        main = dot(masked(sh, vh[:cut], lower), kh[:cut], NN)
        rest = dot(masked(sh[cut:], vh[cut:], col <= row), kh[cut:], NN)
        pq[:cut, cols] = main[:cut]
        pq[cut:, cols] = main[cut:] + rest
        main = dot(masked(vh, sh[HEAD:], upper), qh[HEAD:], NN)
        rest = dot(masked(vh[:HEAD], sh[:HEAD], row <= col), qh[:HEAD], NN)
        pk[:HEAD, cols] = main[:HEAD] + rest
        pk[HEAD:, cols] = main[HEAD:]
        main = dot(masked(kh, qh[HEAD:], upper), sh[HEAD:], NN)
        rest = dot(masked(kh[:HEAD], qh[:HEAD], row <= col), sh[:HEAD], NN)
        pv[:HEAD, cols] = main[:HEAD] + rest
        pv[HEAD:, cols] = main[HEAD:]
        return carry

    actions = {
        "S": states, "R": group_sums, "T": outer_totals, "Z": offsets, "P": block_states, "F": finish,
    }
    for step in schedule():
        if step[0] == "I":
            lax.fori_loop(step[1], step[2], inside, 0)
        else:
            actions[step[0]](step[1])

    for c in range(CHUNKS):
        for copy in stores(c):
            copy.wait()

    def sent(ref, stage):
        pltpu.make_async_copy(ref, ref, send_sem.at[stage]).wait()

    sent(ysend.at[pl.ds(0, CHUNKS * (NY - 1))], 0)
    sent(zsend.at[pl.ds(0, CHUNKS * (nz - 1))], 1)
    for c in range(CHUNKS):
        sent(trecv.at[c, pl.ds(0, no - 1)], 2)
    sent(bsend.at[pl.ds(0, CHUNKS * (nz - 1))], 3)
    sent(psend.at[pl.ds(0, CHUNKS * (NY - 1))], 4)


def solution(mesh):
    no = mesh.shape["outer"]
    nz = mesh.shape["inner"] // NY
    sub = HEAD // nz

    def local(query_rows, key_rows, value_rows, grad_output):
        shape = query_rows.shape
        out = jax.ShapeDtypeStruct(shape, BF16)
        anywhere = pl.BlockSpec(memory_space=pl.ANY)
        return pl.pallas_call(
            functools.partial(kernel, no, nz),
            name="linear_attention_grads",
            out_shape=(out, out, out),
            in_specs=[anywhere] * 4,
            out_specs=(anywhere,) * 3,
            scratch_shapes=(
                [pltpu.VMEM(shape, BF16)] * 5
                + [pltpu.VMEM(shape, F32)] * 3
                + [pltpu.VMEM(shape, BF16)] * 3
                + [
                    pltpu.VMEM((CHUNKS * NY, 2, HEAD, HEAD), BF16),
                    pltpu.VMEM((CHUNKS, NY, 2, HEAD, HEAD), BF16),
                    pltpu.VMEM((CHUNKS * nz, 2, sub, HEAD), BF16),
                    pltpu.VMEM((CHUNKS, nz, 2, sub, HEAD), BF16),
                    pltpu.VMEM((CHUNKS, 2, sub, HEAD), F32),
                    pltpu.VMEM((CHUNKS, no, sub, HEAD), F32),
                    pltpu.VMEM((CHUNKS * nz, 2, sub, HEAD), BF16),
                    pltpu.VMEM((CHUNKS, nz, 2, sub, HEAD), BF16),
                    pltpu.VMEM((CHUNKS * NY, 2, HEAD, HEAD), BF16),
                    pltpu.VMEM((CHUNKS, NY, 2, HEAD, HEAD), BF16),
                    pltpu.SemaphoreType.DMA((CHUNKS, 4)),
                    pltpu.SemaphoreType.DMA((CHUNKS, 3)),
                    pltpu.SemaphoreType.DMA((5,)),
                    pltpu.SemaphoreType.DMA((5, CHUNKS)),
                ]
            ),
            compiler_params=pltpu.CompilerParams(
                collective_id=0, has_side_effects=True, vmem_limit_bytes=48 << 20
            ),
        )(query_rows, key_rows, value_rows, grad_output)

    placed = P(("outer", "inner"), None)
    return jax.shard_map(
        local, mesh=mesh, in_specs=(placed,) * 4, out_specs=(placed,) * 3, check_vma=False
    )
```

```python
import functools

import jax
import jax.numpy as jnp
from jax import lax
from jax.experimental import pallas as pl
from jax.experimental.pallas import tpu as pltpu
from jax.sharding import PartitionSpec as P

MESH = pl.DeviceIdType.MESH
HEADS = 16
HEAD = 128
NY = 4
PARTS = (4, 4, 4, 4)
CHUNKS = len(PARTS)
ORDER = (
    "S0 S1 S2 S3 "
    "I6 R0 I2 R1 "
    "I2 R2 T0 I2 "
    "R3 T1 Z0 I2 "
    "T2 Z1 I2 L0 "
    "T3 P0 Z2 P1 "
    "Z3 P2 P3 F0 "
    "F1 F2 "
)
LIMIT = 90 << 19
START = [sum(PARTS[:c]) for c in range(CHUNKS)]
F32 = jnp.float32
BF16 = jnp.bfloat16

NN = (((1,), (0,)), ((), ()))
NT = (((1,), (1,)), ((), ()))
TN = (((0,), (0,)), ((), ()))


def dot(a, b, dims):
    return lax.dot_general(a, b, dims, preferred_element_type=F32)


def far_first(count):
    return sorted(range(1, count), key=lambda step: -min(step, count - step))


def schedule():
    order = []
    inner = 0
    for step in ORDER.split():
        if step[0] == "I":
            count = int(step[1:])
            order.append(("I", inner, inner + count))
            inner += count
        else:
            order.append((step[0], int(step[1:])))
    return order


def kernel(no, nz, *refs):
    refs = iter(refs)

    def take(count):
        return [next(refs) for _ in range(count)]

    q_hbm, k_hbm, v_hbm, g_hbm = take(4)
    oq, ok, ov, lq, lk, lv, ls, lw, lx, last_states = take(10)
    q, k, v, g, sg, pq, pk, pv = take(8)
    ysend, yrecv, zsend, zrecv, tsend, trecv, bsend, brecv, psend = (take(CHUNKS) for _ in range(9))
    precv = take(CHUNKS - 1)
    in_sem, send_sem, recv_sem = take(3)
    precv.append(last_states)
    length = q.shape[0]
    o = lax.axis_index("outer")
    i = lax.axis_index("inner")
    z = i // NY
    y = i % NY

    ypeers = [lax.rem(y + d, NY) for d in far_first(NY)]
    zpeers = [lax.rem(z + d, nz) for d in far_first(nz)]
    opeers = [lax.rem(o + d, no) for d in far_first(no)]

    def loads(c):
        cols = pl.ds(START[c] * HEAD, PARTS[c] * HEAD)
        return [
            pltpu.make_async_copy(src.at[:, cols], dst.at[:, cols], in_sem.at[c, j])
            for j, (src, dst) in enumerate(((k_hbm, k), (v_hbm, v), (g_hbm, g), (q_hbm, q)))
        ]

    for c in range(CHUNKS):
        for copy in loads(c):
            copy.start()

    barrier = pltpu.get_barrier_semaphore()
    everyone = (
        [(o, z * NY + p) for p in ypeers]
        + [(o, p * NY + y) for p in zpeers]
        + [(p, i) for p in opeers]
    )
    for peer in everyone:
        pl.semaphore_signal(barrier, inc=1, device_id=peer, device_id_type=MESH)

    offset = (o * (nz * NY) + i) * length
    rows = lax.broadcasted_iota(jnp.int32, (length, HEAD), 0) + offset
    scales = lax.rsqrt(rows.astype(F32) + 1.0)

    def send(src, dst, stage, c, peer):
        pltpu.make_async_remote_copy(
            src_ref=src, dst_ref=dst, send_sem=send_sem.at[stage, c], recv_sem=recv_sem.at[stage, c],
            device_id=peer, device_id_type=MESH,
        ).start()

    def arrived(ref, stage, c):
        pltpu.make_async_copy(ref, ref, recv_sem.at[stage, c]).wait()

    def states(c):
        for copy in loads(c):
            copy.wait()
        part = yrecv[c].shape[2]
        for j in range(PARTS[c]):
            cols = pl.ds((START[c] + j) * HEAD, HEAD)
            scaled = (g[:, cols].astype(F32) * scales).astype(BF16)
            sg[:, cols] = scaled
            both = (dot(k[:, cols], v[:, cols], TN), dot(q[:, cols], scaled, TN))
            for kind in range(2):
                for r in range(0, HEAD, part):
                    ysend[c][(j * HEAD + r) // part, kind] = both[kind][r:r + part].astype(BF16)
        if c == 0:
            pl.semaphore_wait(barrier, len(everyone))
        for p in ypeers:
            send(ysend[c].at[p], yrecv[c].at[y], 0, c, (o, z * NY + p))
        yrecv[c][y] = ysend[c][y]

    def group_sums(c):
        arrived(yrecv[c].at[pl.ds(0, NY - 1)], 0, c)
        total = yrecv[c][0].astype(F32)
        for p in range(1, NY):
            total = total + yrecv[c][p].astype(F32)
        sub = total.shape[1] // nz
        for p in range(nz):
            cut = slice(p * sub, (p + 1) * sub)
            zsend[c][p] = jnp.concatenate([total[0, cut], total[1, cut]], axis=0).astype(BF16)
        for p in zpeers:
            send(zsend[c].at[p], zrecv[c].at[z], 1, c, (o, p * NY + y))
        zrecv[c][z] = zsend[c][z]

    def outer_totals(c):
        arrived(zrecv[c].at[pl.ds(0, nz - 1)], 1, c)
        total = zrecv[c][0].astype(F32)
        for p in range(1, nz):
            total = total + zrecv[c][p].astype(F32)
        sub = total.shape[0] // 2
        tsend[c][0] = total[:sub]
        tsend[c][1] = total[sub:]
        for p in opeers:
            kind = jnp.where(p > o, 0, 1)
            send(tsend[c].at[kind], trecv[c].at[o], 2, c, (p, i))
        trecv[c][o] = jnp.zeros((sub, HEAD), F32)

    def offsets(c):
        arrived(trecv[c].at[pl.ds(0, no - 1)], 2, c)
        sub = trecv[c].shape[1]
        before = jnp.zeros((sub, HEAD), F32)
        after = jnp.zeros((sub, HEAD), F32)
        for p in range(no):
            part = trecv[c][p]
            before = before + jnp.where(p < o, part, 0.0)
            after = after + jnp.where(p > o, part, 0.0)
        own = [zrecv[c][p].astype(F32) for p in range(nz)]
        befores, afters = [], []
        for p in range(nz):
            befores.append(before)
            before = before + own[p][:sub]
        for p in reversed(range(nz)):
            afters.append(after)
            after = after + own[p][sub:]
        for p in range(nz):
            bsend[c][p] = jnp.concatenate([befores[p], afters[nz - 1 - p]], axis=0).astype(BF16)
        for p in zpeers:
            send(bsend[c].at[p], brecv[c].at[z], 3, c, (o, p * NY + y))
        brecv[c][z] = bsend[c][z]

    def block_states(c):
        arrived(brecv[c].at[pl.ds(0, nz - 1)], 3, c)
        sub = brecv[c].shape[1] // 2
        pieces = [brecv[c][p].astype(F32) for p in range(nz)]
        before = jnp.concatenate([piece[:sub] for piece in pieces], axis=0)
        after = jnp.concatenate([piece[sub:] for piece in pieces], axis=0)
        for r in range(NY):
            psend[c][r, 0] = before.astype(BF16)
            before = before + yrecv[c][r, 0].astype(F32)
        for r in reversed(range(NY)):
            psend[c][r, 1] = after.astype(BF16)
            after = after + yrecv[c][r, 1].astype(F32)
        for p in ypeers:
            send(psend[c].at[p], precv[c].at[y], 4, c, (o, z * NY + p))
        precv[c][y] = psend[c][y]

    def finish(c):
        arrived(precv[c].at[pl.ds(0, NY - 1)], 4, c)
        part = precv[c].shape[2]
        span = HEAD // part
        for j in range(PARTS[c]):
            cols = pl.ds((START[c] + j) * HEAD, HEAD)
            prefix, suffix = (
                jnp.concatenate([precv[c][j * span + r, kind] for r in range(span)], axis=0)
                for kind in range(2)
            )
            oq[:, cols] = (pq[:, cols] + dot(sg[:, cols], prefix, NT)).astype(BF16)
            ok[:, cols] = (pk[:, cols] + dot(v[:, cols], suffix, NT)).astype(BF16)
            ov[:, cols] = (pv[:, cols] + dot(k[:, cols], suffix, NN)).astype(BF16)

    def leave():
        cols = pl.ds(START[-1] * HEAD, PARTS[-1] * HEAD)
        for dst, src in ((lq, pq), (lk, pk), (lv, pv), (ls, sg), (lw, v), (lx, k)):
            dst[...] = src[:, cols]

    cut = length - HEAD

    def inside(head, carry):
        cols = pl.ds(pl.multiple_of(head * HEAD, HEAD), HEAD)
        kh, vh, qh, sh = k[:, cols], v[:, cols], q[:, cols], sg[:, cols]
        first = lax.broadcasted_iota(jnp.int32, (length, cut), 0)
        second = lax.broadcasted_iota(jnp.int32, (length, cut), 1)
        lower = second <= first
        upper = first <= second + HEAD
        row = lax.broadcasted_iota(jnp.int32, (HEAD, HEAD), 0)
        col = lax.broadcasted_iota(jnp.int32, (HEAD, HEAD), 1)

        def masked(a, b, mask):
            return jnp.where(mask, dot(a, b, NT), 0.0).astype(BF16)

        main = dot(masked(sh, vh[:cut], lower), kh[:cut], NN)
        rest = dot(masked(sh[cut:], vh[cut:], col <= row), kh[cut:], NN)
        pq[:cut, cols] = main[:cut]
        pq[cut:, cols] = main[cut:] + rest
        main = dot(masked(vh, sh[HEAD:], upper), qh[HEAD:], NN)
        rest = dot(masked(vh[:HEAD], sh[:HEAD], row <= col), qh[:HEAD], NN)
        pk[:HEAD, cols] = main[:HEAD] + rest
        pk[HEAD:, cols] = main[HEAD:]
        main = dot(masked(kh, qh[HEAD:], upper), sh[HEAD:], NN)
        rest = dot(masked(kh[:HEAD], qh[:HEAD], row <= col), sh[:HEAD], NN)
        pv[:HEAD, cols] = main[:HEAD] + rest
        pv[HEAD:, cols] = main[HEAD:]
        return carry

    actions = {
        "S": states, "R": group_sums, "T": outer_totals, "Z": offsets, "P": block_states, "F": finish,
    }
    for step in schedule():
        if step[0] == "I":
            lax.fori_loop(step[1], step[2], inside, 0)
        elif step[0] == "L":
            leave()
        else:
            actions[step[0]](step[1])

    arrived(last_states.at[pl.ds(0, NY - 1)], 4, CHUNKS - 1)
    for c in range(CHUNKS):
        for stage, (ref, count) in enumerate(
            ((ysend, NY), (zsend, nz), (trecv, no), (bsend, nz), (psend, NY))
        ):
            done = ref[c].at[pl.ds(0, count - 1)]
            pltpu.make_async_copy(done, done, send_sem.at[stage, c]).wait()


def outputs(oq, ok, ov, lq, lk, lv, ls, lw, lx, states, oq_hbm, ok_hbm, ov_hbm, fq, fk, fv, sem):
    early = pl.ds(0, START[-1] * HEAD)
    late = pl.ds(START[-1] * HEAD, PARTS[-1] * HEAD)
    copies = [
        pltpu.make_async_copy(src.at[:, early], dst.at[:, early], sem.at[0, j])
        for j, (src, dst) in enumerate(((oq, oq_hbm), (ok, ok_hbm), (ov, ov_hbm)))
    ]
    for copy in copies:
        copy.start()
    span = HEAD // states.shape[2]
    sides = [[], []]
    for j in range(PARTS[-1]):
        for kind in range(2):
            sides[kind].append(jnp.concatenate([states[j * span + r, kind] for r in range(span)], axis=0))
    plan = (
        (fq, lq, ls, sides[0], NT, oq_hbm), (fk, lk, lw, sides[1], NT, ok_hbm), (fv, lv, lx, sides[1], NN, ov_hbm)
    )
    for place, (full, part, left, side, dims, out) in enumerate(plan):
        for j in range(PARTS[-1]):
            cols = pl.ds(j * HEAD, HEAD)
            full[:, cols] = (part[:, cols] + dot(left[:, cols], side[j], dims)).astype(BF16)
        copy = pltpu.make_async_copy(full, out.at[:, late], sem.at[1, place])
        copy.start()
        copies.append(copy)
    for copy in copies:
        copy.wait()


def solution(mesh):
    no = mesh.shape["outer"]
    nz = mesh.shape["inner"] // NY

    def local(query_rows, key_rows, value_rows, grad_output):
        shape = query_rows.shape
        out = jax.ShapeDtypeStruct(shape, BF16)
        anywhere = pl.BlockSpec(memory_space=pltpu.HBM)
        inside = pl.BlockSpec(memory_space=pltpu.VMEM)
        rows = [heads * HEAD // NY for heads in PARTS]

        def buffers(make):
            return [make(count) for count in rows]

        wide = buffers(lambda count: pltpu.VMEM((NY, 2, count, HEAD), BF16))
        thin = buffers(lambda count: pltpu.VMEM((nz, 2 * (count // nz), HEAD), BF16))
        length, tail = shape[0], PARTS[-1] * HEAD
        narrow = jax.ShapeDtypeStruct((length, tail), BF16)
        sums = jax.ShapeDtypeStruct((length, tail), F32)
        last = jax.ShapeDtypeStruct((NY, 2, rows[-1], HEAD), BF16)
        held = pl.pallas_call(
            functools.partial(kernel, no, nz),
            name="linear_attention_grads",
            out_shape=(out,) * 3 + (sums,) * 3 + (narrow,) * 3 + (last,),
            in_specs=[anywhere] * 4,
            out_specs=(inside,) * 10,
            scratch_shapes=(
                [pltpu.VMEM(shape, BF16)] * 5
                + [pltpu.VMEM(shape, F32)] * 3
                + wide * 2
                + thin * 2
                + buffers(lambda count: pltpu.VMEM((2, count // nz, HEAD), F32))
                + buffers(lambda count: pltpu.VMEM((no, count // nz, HEAD), F32))
                + thin * 2
                + wide
                + wide[:-1]
                + [
                    pltpu.SemaphoreType.DMA((CHUNKS, 4)),
                    pltpu.SemaphoreType.DMA((5, CHUNKS)),
                    pltpu.SemaphoreType.DMA((5, CHUNKS)),
                ]
            ),
            compiler_params=pltpu.CompilerParams(
                collective_id=0, has_side_effects=True, vmem_limit_bytes=LIMIT
            ),
        )(query_rows, key_rows, value_rows, grad_output)
        return pl.pallas_call(
            outputs,
            name="write_grads",
            out_shape=(out, out, out),
            in_specs=[inside] * 10,
            out_specs=(anywhere,) * 3,
            scratch_shapes=[pltpu.VMEM((length, tail), BF16)] * 3 + [pltpu.SemaphoreType.DMA((2, 3))],
            compiler_params=pltpu.CompilerParams(vmem_limit_bytes=8 << 20),
        )(*held)

    placed = P(("outer", "inner"), None)
    return jax.shard_map(
        local, mesh=mesh, in_specs=(placed,) * 4, out_specs=(placed,) * 3, check_vma=False
    )
```

```python
import functools

import jax
import jax.numpy as jnp
from jax import lax
from jax.experimental import pallas as pl
from jax.experimental.pallas import tpu as pltpu
from jax.sharding import PartitionSpec as P

MESH = pl.DeviceIdType.MESH
HEADS = 16
HEAD = 128
NY = 4
PARTS = (4, 4, 4, 4)
CHUNKS = len(PARTS)
ORDER = (
    "S0", "S1", "S2", "S3", "I6", "R0", "I2", "R1", "I2", "R2", "T0", "I2",
    "R3", "T1", "Z0", "I2", "T2", "Z1", "I2", "L0", "T3", "P0", "Z2", "P1",
    "Z3", "P2", "P3", "F0", "F1", "F2",
)
LIMIT = 90 << 19
START = [sum(PARTS[:c]) for c in range(CHUNKS)]
F32 = jnp.float32
BF16 = jnp.bfloat16

NN = (((1,), (0,)), ((), ()))
NT = (((1,), (1,)), ((), ()))
TN = (((0,), (0,)), ((), ()))


def dot(a, b, dims):
    return lax.dot_general(a, b, dims, preferred_element_type=F32)


def far_first(count):
    return sorted(range(1, count), key=lambda step: -min(step, count - step))


def schedule():
    order = []
    inner = 0
    for step in ORDER:
        if step[0] == "I":
            count = int(step[1:])
            order.append(("I", inner, inner + count))
            inner += count
        else:
            order.append((step[0], int(step[1:])))
    return order


def kernel(no, nz, *refs):
    refs = iter(refs)

    def take(count):
        return [next(refs) for _ in range(count)]

    q_hbm, k_hbm, v_hbm, g_hbm = take(4)
    oq, ok, ov, lq, lk, lv, ls, lw, lx, last_states = take(10)
    q, k, v, g, sg, pq, pk, pv = take(8)
    ysend, yrecv, zsend, zrecv, tsend, trecv, bsend, brecv, psend = (take(CHUNKS) for _ in range(9))
    precv = take(CHUNKS - 1)
    in_sem, send_sem, recv_sem = take(3)
    precv.append(last_states)
    length = q.shape[0]
    o = lax.axis_index("outer")
    i = lax.axis_index("inner")
    z = i // NY
    y = i % NY

    ypeers = [lax.rem(y + d, NY) for d in far_first(NY)]
    zpeers = [lax.rem(z + d, nz) for d in far_first(nz)]
    opeers = [lax.rem(o + d, no) for d in far_first(no)]

    def loads(c):
        cols = pl.ds(START[c] * HEAD, PARTS[c] * HEAD)
        return [
            pltpu.make_async_copy(src.at[:, cols], dst.at[:, cols], in_sem.at[c, j])
            for j, (src, dst) in enumerate(((k_hbm, k), (v_hbm, v), (g_hbm, g), (q_hbm, q)))
        ]

    for c in range(CHUNKS):
        for copy in loads(c):
            copy.start()

    barrier = pltpu.get_barrier_semaphore()
    everyone = (
        [(o, z * NY + p) for p in ypeers]
        + [(o, p * NY + y) for p in zpeers]
        + [(p, i) for p in opeers]
    )
    for peer in everyone:
        pl.semaphore_signal(barrier, inc=1, device_id=peer, device_id_type=MESH)

    offset = (o * (nz * NY) + i) * length
    rows = lax.broadcasted_iota(jnp.int32, (length, HEAD), 0) + offset
    scales = lax.rsqrt(rows.astype(F32) + 1.0)

    def send(src, dst, stage, c, peer):
        pltpu.make_async_remote_copy(
            src_ref=src, dst_ref=dst, send_sem=send_sem.at[stage, c], recv_sem=recv_sem.at[stage, c],
            device_id=peer, device_id_type=MESH,
        ).start()

    def arrived(ref, stage, c):
        pltpu.make_async_copy(ref, ref, recv_sem.at[stage, c]).wait()

    def states(c):
        for copy in loads(c):
            copy.wait()
        part = yrecv[c].shape[2]
        for j in range(PARTS[c]):
            cols = pl.ds((START[c] + j) * HEAD, HEAD)
            scaled = (g[:, cols].astype(F32) * scales).astype(BF16)
            sg[:, cols] = scaled
            both = (dot(k[:, cols], v[:, cols], TN), dot(q[:, cols], scaled, TN))
            for kind in range(2):
                for r in range(0, HEAD, part):
                    ysend[c][(j * HEAD + r) // part, kind] = both[kind][r:r + part].astype(BF16)
        if c == 0:
            pl.semaphore_wait(barrier, len(everyone))
        for p in ypeers:
            send(ysend[c].at[p], yrecv[c].at[y], 0, c, (o, z * NY + p))
        yrecv[c][y] = ysend[c][y]

    def group_sums(c):
        arrived(yrecv[c].at[pl.ds(0, NY - 1)], 0, c)
        total = yrecv[c][0].astype(F32)
        for p in range(1, NY):
            total = total + yrecv[c][p].astype(F32)
        sub = total.shape[1] // nz
        for p in range(nz):
            cut = slice(p * sub, (p + 1) * sub)
            zsend[c][p] = jnp.concatenate([total[0, cut], total[1, cut]], axis=0).astype(BF16)
        for p in zpeers:
            send(zsend[c].at[p], zrecv[c].at[z], 1, c, (o, p * NY + y))
        zrecv[c][z] = zsend[c][z]

    def outer_totals(c):
        arrived(zrecv[c].at[pl.ds(0, nz - 1)], 1, c)
        total = zrecv[c][0].astype(F32)
        for p in range(1, nz):
            total = total + zrecv[c][p].astype(F32)
        sub = total.shape[0] // 2
        tsend[c][0] = total[:sub]
        tsend[c][1] = total[sub:]
        for p in opeers:
            kind = jnp.where(p > o, 0, 1)
            send(tsend[c].at[kind], trecv[c].at[o], 2, c, (p, i))
        trecv[c][o] = jnp.zeros((sub, HEAD), F32)

    def offsets(c):
        arrived(trecv[c].at[pl.ds(0, no - 1)], 2, c)
        sub = trecv[c].shape[1]
        before = jnp.zeros((sub, HEAD), F32)
        after = jnp.zeros((sub, HEAD), F32)
        for p in range(no):
            part = trecv[c][p]
            before = before + jnp.where(p < o, part, 0.0)
            after = after + jnp.where(p > o, part, 0.0)
        own = [zrecv[c][p].astype(F32) for p in range(nz)]
        befores, afters = [], []
        for p in range(nz):
            befores.append(before)
            before = before + own[p][:sub]
        for p in reversed(range(nz)):
            afters.append(after)
            after = after + own[p][sub:]
        for p in range(nz):
            bsend[c][p] = jnp.concatenate([befores[p], afters[nz - 1 - p]], axis=0).astype(BF16)
        for p in zpeers:
            send(bsend[c].at[p], brecv[c].at[z], 3, c, (o, p * NY + y))
        brecv[c][z] = bsend[c][z]

    def block_states(c):
        arrived(brecv[c].at[pl.ds(0, nz - 1)], 3, c)
        sub = brecv[c].shape[1] // 2
        pieces = [brecv[c][p].astype(F32) for p in range(nz)]
        before = jnp.concatenate([piece[:sub] for piece in pieces], axis=0)
        after = jnp.concatenate([piece[sub:] for piece in pieces], axis=0)
        for r in range(NY):
            psend[c][r, 0] = before.astype(BF16)
            before = before + yrecv[c][r, 0].astype(F32)
        for r in reversed(range(NY)):
            psend[c][r, 1] = after.astype(BF16)
            after = after + yrecv[c][r, 1].astype(F32)
        for p in ypeers:
            send(psend[c].at[p], precv[c].at[y], 4, c, (o, z * NY + p))
        precv[c][y] = psend[c][y]

    def finish(c):
        arrived(precv[c].at[pl.ds(0, NY - 1)], 4, c)
        part = precv[c].shape[2]
        span = HEAD // part
        for j in range(PARTS[c]):
            cols = pl.ds((START[c] + j) * HEAD, HEAD)
            prefix, suffix = (
                jnp.concatenate([precv[c][j * span + r, kind] for r in range(span)], axis=0)
                for kind in range(2)
            )
            oq[:, cols] = (pq[:, cols] + dot(sg[:, cols], prefix, NT)).astype(BF16)
            ok[:, cols] = (pk[:, cols] + dot(v[:, cols], suffix, NT)).astype(BF16)
            ov[:, cols] = (pv[:, cols] + dot(k[:, cols], suffix, NN)).astype(BF16)

    def leave():
        cols = pl.ds(START[-1] * HEAD, PARTS[-1] * HEAD)
        for dst, src in ((lq, pq), (lk, pk), (lv, pv), (ls, sg), (lw, v), (lx, k)):
            dst[...] = src[:, cols]

    cut = length - HEAD

    def inside(head, carry):
        cols = pl.ds(pl.multiple_of(head * HEAD, HEAD), HEAD)
        kh, vh, qh, sh = k[:, cols], v[:, cols], q[:, cols], sg[:, cols]
        first = lax.broadcasted_iota(jnp.int32, (length, cut), 0)
        second = lax.broadcasted_iota(jnp.int32, (length, cut), 1)
        lower = second <= first
        upper = first <= second + HEAD
        row = lax.broadcasted_iota(jnp.int32, (HEAD, HEAD), 0)
        col = lax.broadcasted_iota(jnp.int32, (HEAD, HEAD), 1)

        def masked(a, b, mask):
            return jnp.where(mask, dot(a, b, NT), 0.0).astype(BF16)

        main = dot(masked(sh, vh[:cut], lower), kh[:cut], NN)
        rest = dot(masked(sh[cut:], vh[cut:], col <= row), kh[cut:], NN)
        pq[:cut, cols] = main[:cut]
        pq[cut:, cols] = main[cut:] + rest
        main = dot(masked(vh, sh[HEAD:], upper), qh[HEAD:], NN)
        rest = dot(masked(vh[:HEAD], sh[:HEAD], row <= col), qh[:HEAD], NN)
        pk[:HEAD, cols] = main[:HEAD] + rest
        pk[HEAD:, cols] = main[HEAD:]
        main = dot(masked(kh, qh[HEAD:], upper), sh[HEAD:], NN)
        rest = dot(masked(kh[:HEAD], qh[:HEAD], row <= col), sh[:HEAD], NN)
        pv[:HEAD, cols] = main[:HEAD] + rest
        pv[HEAD:, cols] = main[HEAD:]
        return carry

    actions = {
        "S": states, "R": group_sums, "T": outer_totals, "Z": offsets, "P": block_states, "F": finish,
    }
    for step in schedule():
        if step[0] == "I":
            lax.fori_loop(step[1], step[2], inside, 0)
        elif step[0] == "L":
            leave()
        else:
            actions[step[0]](step[1])

    arrived(last_states.at[pl.ds(0, NY - 1)], 4, CHUNKS - 1)
    for c in range(CHUNKS):
        for stage, (ref, count) in enumerate(
            ((ysend, NY), (zsend, nz), (trecv, no), (bsend, nz), (psend, NY))
        ):
            done = ref[c].at[pl.ds(0, count - 1)]
            pltpu.make_async_copy(done, done, send_sem.at[stage, c]).wait()


def outputs(oq, ok, ov, lq, lk, lv, ls, lw, lx, states, oq_hbm, ok_hbm, ov_hbm, fq, fk, fv, sem):
    early = pl.ds(0, START[-1] * HEAD)
    late = pl.ds(START[-1] * HEAD, PARTS[-1] * HEAD)
    copies = [
        pltpu.make_async_copy(src.at[:, early], dst.at[:, early], sem.at[0, j])
        for j, (src, dst) in enumerate(((oq, oq_hbm), (ok, ok_hbm), (ov, ov_hbm)))
    ]
    for copy in copies:
        copy.start()
    span = HEAD // states.shape[2]
    sides = [[], []]
    for j in range(PARTS[-1]):
        for kind in range(2):
            sides[kind].append(jnp.concatenate([states[j * span + r, kind] for r in range(span)], axis=0))
    plan = (
        (fq, lq, ls, sides[0], NT, oq_hbm), (fk, lk, lw, sides[1], NT, ok_hbm), (fv, lv, lx, sides[1], NN, ov_hbm)
    )
    for place, (full, part, left, side, dims, out) in enumerate(plan):
        for j in range(PARTS[-1]):
            cols = pl.ds(j * HEAD, HEAD)
            full[:, cols] = (part[:, cols] + dot(left[:, cols], side[j], dims)).astype(BF16)
        copy = pltpu.make_async_copy(full, out.at[:, late], sem.at[1, place])
        copy.start()
        copies.append(copy)
    for copy in copies:
        copy.wait()


def solution(mesh):
    no = mesh.shape["outer"]
    nz = mesh.shape["inner"] // NY

    def local(query_rows, key_rows, value_rows, grad_output):
        shape = query_rows.shape
        out = jax.ShapeDtypeStruct(shape, BF16)
        anywhere = pl.BlockSpec(memory_space=pltpu.HBM)
        inside = pl.BlockSpec(memory_space=pltpu.VMEM)
        rows = [heads * HEAD // NY for heads in PARTS]

        def buffers(make):
            return [make(count) for count in rows]

        wide = buffers(lambda count: pltpu.VMEM((NY, 2, count, HEAD), BF16))
        thin = buffers(lambda count: pltpu.VMEM((nz, 2 * (count // nz), HEAD), BF16))
        length, tail = shape[0], PARTS[-1] * HEAD
        narrow = jax.ShapeDtypeStruct((length, tail), BF16)
        sums = jax.ShapeDtypeStruct((length, tail), F32)
        last = jax.ShapeDtypeStruct((NY, 2, rows[-1], HEAD), BF16)
        held = pl.pallas_call(
            functools.partial(kernel, no, nz),
            name="linear_attention_grads",
            out_shape=(out,) * 3 + (sums,) * 3 + (narrow,) * 3 + (last,),
            in_specs=[anywhere] * 4,
            out_specs=(inside,) * 10,
            scratch_shapes=(
                [pltpu.VMEM(shape, BF16)] * 5
                + [pltpu.VMEM(shape, F32)] * 3
                + wide * 2
                + thin * 2
                + buffers(lambda count: pltpu.VMEM((2, count // nz, HEAD), F32))
                + buffers(lambda count: pltpu.VMEM((no, count // nz, HEAD), F32))
                + thin * 2
                + wide
                + wide[:-1]
                + [
                    pltpu.SemaphoreType.DMA((CHUNKS, 4)),
                    pltpu.SemaphoreType.DMA((5, CHUNKS)),
                    pltpu.SemaphoreType.DMA((5, CHUNKS)),
                ]
            ),
            compiler_params=pltpu.CompilerParams(
                collective_id=0, has_side_effects=True, vmem_limit_bytes=LIMIT
            ),
        )(query_rows, key_rows, value_rows, grad_output)
        return pl.pallas_call(
            outputs,
            name="write_grads",
            out_shape=(out, out, out),
            in_specs=[inside] * 10,
            out_specs=(anywhere,) * 3,
            scratch_shapes=[pltpu.VMEM((length, tail), BF16)] * 3 + [pltpu.SemaphoreType.DMA((2, 3))],
            compiler_params=pltpu.CompilerParams(vmem_limit_bytes=8 << 20),
        )(*held)

    placed = P(("outer", "inner"), None)
    return jax.shard_map(
        local, mesh=mesh, in_specs=(placed,) * 4, out_specs=(placed,) * 3, check_vma=False
    )
```

```python
import functools

import jax
import jax.numpy as jnp
from jax import lax
from jax.experimental import pallas as pl
from jax.experimental.pallas import tpu as pltpu
from jax.sharding import PartitionSpec as P

MESH = pl.DeviceIdType.MESH
HEADS = 16
HEAD = 128
NY = 4
PARTS = (2, 2, 4, 4, 4)
CHUNKS = len(PARTS)
ORDER = (
    "S0", "S1", "S2", "S3", "S4", "I3", "R0", "R1", "I3", "R2", "I1", "T0",
    "I1", "R3", "T1", "I1", "Z0", "R4", "T2", "Z1", "I1", "T3", "I1", "P0",
    "Z2", "T4", "P1", "I1", "Z3", "I2", "P2", "Z4", "I2", "L0", "P3", "P4",
    "F0", "F1", "F2", "F3",
)
LIMIT = 90 << 19
START = [sum(PARTS[:c]) for c in range(CHUNKS)]
F32 = jnp.float32
BF16 = jnp.bfloat16

NN = (((1,), (0,)), ((), ()))
NT = (((1,), (1,)), ((), ()))
TN = (((0,), (0,)), ((), ()))


def dot(a, b, dims):
    return lax.dot_general(a, b, dims, preferred_element_type=F32)


def far_first(count):
    return sorted(range(1, count), key=lambda step: -min(step, count - step))


def schedule():
    order = []
    inner = 0
    for step in ORDER:
        if step[0] == "I":
            count = int(step[1:])
            order.append(("I", inner, inner + count))
            inner += count
        else:
            order.append((step[0], int(step[1:])))
    return order


def kernel(no, nz, *refs):
    refs = iter(refs)

    def take(count):
        return [next(refs) for _ in range(count)]

    q_hbm, k_hbm, v_hbm, g_hbm = take(4)
    oq, ok, ov, lq, lk, lv, ls, lw, lx, last_states = take(10)
    q, k, v, g, sg, pq, pk, pv = take(8)
    ysend, yrecv, zsend, zrecv, tsend, trecv, bsend, brecv, psend = (take(CHUNKS) for _ in range(9))
    precv = take(CHUNKS - 1)
    in_sem, send_sem, recv_sem = take(3)
    precv.append(last_states)
    length = q.shape[0]
    o = lax.axis_index("outer")
    i = lax.axis_index("inner")
    z = i // NY
    y = i % NY

    ypeers = [lax.rem(y + d, NY) for d in far_first(NY)]
    zpeers = [lax.rem(z + d, nz) for d in far_first(nz)]
    opeers = [lax.rem(o + d, no) for d in far_first(no)]

    def loads(c):
        cols = pl.ds(START[c] * HEAD, PARTS[c] * HEAD)
        return [
            pltpu.make_async_copy(src.at[:, cols], dst.at[:, cols], in_sem.at[c, j])
            for j, (src, dst) in enumerate(((k_hbm, k), (v_hbm, v), (g_hbm, g), (q_hbm, q)))
        ]

    for copy in loads(0):
        copy.start()

    barrier = pltpu.get_barrier_semaphore()
    everyone = (
        [(o, p * NY + y) for p in zpeers]
        + [(p, i) for p in opeers]
        + [(o, z * NY + p) for p in ypeers]
    )
    for peer in everyone:
        pl.semaphore_signal(barrier, inc=1, device_id=peer, device_id_type=MESH)
    for c in range(1, CHUNKS):
        for copy in loads(c):
            copy.start()

    offset = (o * (nz * NY) + i) * length
    rows = lax.broadcasted_iota(jnp.int32, (length, HEAD), 0) + offset
    scales = lax.rsqrt(rows.astype(F32) + 1.0)

    def send(src, dst, stage, c, peer):
        pltpu.make_async_remote_copy(
            src_ref=src, dst_ref=dst, send_sem=send_sem.at[stage, c], recv_sem=recv_sem.at[stage, c],
            device_id=peer, device_id_type=MESH,
        ).start()

    def arrived(ref, stage, c):
        pltpu.make_async_copy(ref, ref, recv_sem.at[stage, c]).wait()

    def states(c):
        for copy in loads(c):
            copy.wait()
        part = yrecv[c].shape[2]
        for j in range(PARTS[c]):
            cols = pl.ds((START[c] + j) * HEAD, HEAD)
            scaled = (g[:, cols].astype(F32) * scales).astype(BF16)
            sg[:, cols] = scaled
            both = (dot(k[:, cols], v[:, cols], TN), dot(q[:, cols], scaled, TN))
            for kind in range(2):
                for r in range(0, HEAD, part):
                    ysend[c][(j * HEAD + r) // part, kind] = both[kind][r:r + part].astype(BF16)
        if c == 0:
            pl.semaphore_wait(barrier, len(everyone))
        for p in ypeers:
            send(ysend[c].at[p], yrecv[c].at[y], 0, c, (o, z * NY + p))
        yrecv[c][y] = ysend[c][y]

    def group_sums(c):
        arrived(yrecv[c].at[pl.ds(0, NY - 1)], 0, c)
        total = yrecv[c][0].astype(F32)
        for p in range(1, NY):
            total = total + yrecv[c][p].astype(F32)
        sub = total.shape[1] // nz
        for p in range(nz):
            cut = slice(p * sub, (p + 1) * sub)
            zsend[c][p] = jnp.concatenate([total[0, cut], total[1, cut]], axis=0).astype(BF16)
        for p in zpeers:
            send(zsend[c].at[p], zrecv[c].at[z], 1, c, (o, p * NY + y))
        zrecv[c][z] = zsend[c][z]

    def outer_totals(c):
        arrived(zrecv[c].at[pl.ds(0, nz - 1)], 1, c)
        total = zrecv[c][0].astype(F32)
        for p in range(1, nz):
            total = total + zrecv[c][p].astype(F32)
        sub = total.shape[0] // 2
        tsend[c][0] = total[:sub]
        tsend[c][1] = total[sub:]
        for p in opeers:
            kind = jnp.where(p > o, 0, 1)
            send(tsend[c].at[kind], trecv[c].at[o], 2, c, (p, i))
        trecv[c][o] = jnp.zeros((sub, HEAD), F32)

    def offsets(c):
        arrived(trecv[c].at[pl.ds(0, no - 1)], 2, c)
        sub = trecv[c].shape[1]
        before = jnp.zeros((sub, HEAD), F32)
        after = jnp.zeros((sub, HEAD), F32)
        for p in range(no):
            part = trecv[c][p]
            before = before + jnp.where(p < o, part, 0.0)
            after = after + jnp.where(p > o, part, 0.0)
        own = [zrecv[c][p].astype(F32) for p in range(nz)]
        befores, afters = [], []
        for p in range(nz):
            befores.append(before)
            before = before + own[p][:sub]
        for p in reversed(range(nz)):
            afters.append(after)
            after = after + own[p][sub:]
        for p in range(nz):
            bsend[c][p] = jnp.concatenate([befores[p], afters[nz - 1 - p]], axis=0).astype(BF16)
        for p in zpeers:
            send(bsend[c].at[p], brecv[c].at[z], 3, c, (o, p * NY + y))
        brecv[c][z] = bsend[c][z]

    def block_states(c):
        arrived(brecv[c].at[pl.ds(0, nz - 1)], 3, c)
        sub = brecv[c].shape[1] // 2
        pieces = [brecv[c][p].astype(F32) for p in range(nz)]
        before = jnp.concatenate([piece[:sub] for piece in pieces], axis=0)
        after = jnp.concatenate([piece[sub:] for piece in pieces], axis=0)
        for r in range(NY):
            psend[c][r, 0] = before.astype(BF16)
            before = before + yrecv[c][r, 0].astype(F32)
        for r in reversed(range(NY)):
            psend[c][r, 1] = after.astype(BF16)
            after = after + yrecv[c][r, 1].astype(F32)
        for p in ypeers:
            send(psend[c].at[p], precv[c].at[y], 4, c, (o, z * NY + p))
        precv[c][y] = psend[c][y]

    def finish(c):
        arrived(precv[c].at[pl.ds(0, NY - 1)], 4, c)
        part = precv[c].shape[2]
        span = HEAD // part
        for j in range(PARTS[c]):
            cols = pl.ds((START[c] + j) * HEAD, HEAD)
            prefix, suffix = (
                jnp.concatenate([precv[c][j * span + r, kind] for r in range(span)], axis=0)
                for kind in range(2)
            )
            oq[:, cols] = (pq[:, cols] + dot(sg[:, cols], prefix, NT)).astype(BF16)
            ok[:, cols] = (pk[:, cols] + dot(v[:, cols], suffix, NT)).astype(BF16)
            ov[:, cols] = (pv[:, cols] + dot(k[:, cols], suffix, NN)).astype(BF16)

    def leave():
        cols = pl.ds(START[-1] * HEAD, PARTS[-1] * HEAD)
        for dst, src in ((lq, pq), (lk, pk), (lv, pv), (ls, sg), (lw, v), (lx, k)):
            dst[...] = src[:, cols]

    cut = length - HEAD

    def inside(head, carry):
        cols = pl.ds(pl.multiple_of(head * HEAD, HEAD), HEAD)
        kh, vh, qh, sh = k[:, cols], v[:, cols], q[:, cols], sg[:, cols]
        first = lax.broadcasted_iota(jnp.int32, (length, cut), 0)
        second = lax.broadcasted_iota(jnp.int32, (length, cut), 1)
        lower = second <= first
        upper = first <= second + HEAD
        row = lax.broadcasted_iota(jnp.int32, (HEAD, HEAD), 0)
        col = lax.broadcasted_iota(jnp.int32, (HEAD, HEAD), 1)

        def masked(a, b, mask):
            return jnp.where(mask, dot(a, b, NT), 0.0).astype(BF16)

        main = dot(masked(sh, vh[:cut], lower), kh[:cut], NN)
        rest = dot(masked(sh[cut:], vh[cut:], col <= row), kh[cut:], NN)
        pq[:cut, cols] = main[:cut]
        pq[cut:, cols] = main[cut:] + rest
        main = dot(masked(vh, sh[HEAD:], upper), qh[HEAD:], NN)
        rest = dot(masked(vh[:HEAD], sh[:HEAD], row <= col), qh[:HEAD], NN)
        pk[:HEAD, cols] = main[:HEAD] + rest
        pk[HEAD:, cols] = main[HEAD:]
        main = dot(masked(kh, qh[HEAD:], upper), sh[HEAD:], NN)
        rest = dot(masked(kh[:HEAD], qh[:HEAD], row <= col), sh[:HEAD], NN)
        pv[:HEAD, cols] = main[:HEAD] + rest
        pv[HEAD:, cols] = main[HEAD:]
        return carry

    actions = {
        "S": states, "R": group_sums, "T": outer_totals, "Z": offsets, "P": block_states, "F": finish,
    }
    for step in schedule():
        if step[0] == "I":
            lax.fori_loop(step[1], step[2], inside, 0)
        elif step[0] == "L":
            leave()
        else:
            actions[step[0]](step[1])

    arrived(last_states.at[pl.ds(0, NY - 1)], 4, CHUNKS - 1)
    for c in range(CHUNKS):
        for stage, (ref, count) in enumerate(
            ((ysend, NY), (zsend, nz), (trecv, no), (bsend, nz), (psend, NY))
        ):
            done = ref[c].at[pl.ds(0, count - 1)]
            pltpu.make_async_copy(done, done, send_sem.at[stage, c]).wait()


def outputs(oq, ok, ov, lq, lk, lv, ls, lw, lx, states, oq_hbm, ok_hbm, ov_hbm, fq, fk, fv, sem):
    early = pl.ds(0, START[-1] * HEAD)
    late = pl.ds(START[-1] * HEAD, PARTS[-1] * HEAD)
    copies = [
        pltpu.make_async_copy(src.at[:, early], dst.at[:, early], sem.at[0, j])
        for j, (src, dst) in enumerate(((oq, oq_hbm), (ok, ok_hbm), (ov, ov_hbm)))
    ]
    for copy in copies:
        copy.start()
    span = HEAD // states.shape[2]
    sides = [[], []]
    for j in range(PARTS[-1]):
        for kind in range(2):
            sides[kind].append(jnp.concatenate([states[j * span + r, kind] for r in range(span)], axis=0))
    plan = (
        (fq, lq, ls, sides[0], NT, oq_hbm), (fk, lk, lw, sides[1], NT, ok_hbm), (fv, lv, lx, sides[1], NN, ov_hbm)
    )
    for place, (full, part, left, side, dims, out) in enumerate(plan):
        for j in range(PARTS[-1]):
            cols = pl.ds(j * HEAD, HEAD)
            full[:, cols] = (part[:, cols] + dot(left[:, cols], side[j], dims)).astype(BF16)
        copy = pltpu.make_async_copy(full, out.at[:, late], sem.at[1, place])
        copy.start()
        copies.append(copy)
    for copy in copies:
        copy.wait()


def solution(mesh):
    no = mesh.shape["outer"]
    nz = mesh.shape["inner"] // NY

    def local(query_rows, key_rows, value_rows, grad_output):
        shape = query_rows.shape
        out = jax.ShapeDtypeStruct(shape, BF16)
        anywhere = pl.BlockSpec(memory_space=pltpu.HBM)
        inside = pl.BlockSpec(memory_space=pltpu.VMEM)
        rows = [heads * HEAD // NY for heads in PARTS]

        def buffers(make):
            return [make(count) for count in rows]

        wide = buffers(lambda count: pltpu.VMEM((NY, 2, count, HEAD), BF16))
        thin = buffers(lambda count: pltpu.VMEM((nz, 2 * (count // nz), HEAD), BF16))
        length, tail = shape[0], PARTS[-1] * HEAD
        narrow = jax.ShapeDtypeStruct((length, tail), BF16)
        sums = jax.ShapeDtypeStruct((length, tail), F32)
        last = jax.ShapeDtypeStruct((NY, 2, rows[-1], HEAD), BF16)
        held = pl.pallas_call(
            functools.partial(kernel, no, nz),
            name="linear_attention_grads",
            out_shape=(out,) * 3 + (sums,) * 3 + (narrow,) * 3 + (last,),
            in_specs=[anywhere] * 4,
            out_specs=(inside,) * 10,
            scratch_shapes=(
                [pltpu.VMEM(shape, BF16)] * 5
                + [pltpu.VMEM(shape, F32)] * 3
                + wide * 2
                + thin * 2
                + buffers(lambda count: pltpu.VMEM((2, count // nz, HEAD), F32))
                + buffers(lambda count: pltpu.VMEM((no, count // nz, HEAD), F32))
                + thin * 2
                + wide
                + wide[:-1]
                + [
                    pltpu.SemaphoreType.DMA((CHUNKS, 4)),
                    pltpu.SemaphoreType.DMA((5, CHUNKS)),
                    pltpu.SemaphoreType.DMA((5, CHUNKS)),
                ]
            ),
            compiler_params=pltpu.CompilerParams(
                collective_id=0, has_side_effects=True, vmem_limit_bytes=LIMIT
            ),
        )(query_rows, key_rows, value_rows, grad_output)
        return pl.pallas_call(
            outputs,
            name="write_grads",
            out_shape=(out, out, out),
            in_specs=[inside] * 10,
            out_specs=(anywhere,) * 3,
            scratch_shapes=[pltpu.VMEM((length, tail), BF16)] * 3 + [pltpu.SemaphoreType.DMA((2, 3))],
            compiler_params=pltpu.CompilerParams(vmem_limit_bytes=8 << 20),
        )(*held)

    placed = P(("outer", "inner"), None)
    return jax.shard_map(
        local, mesh=mesh, in_specs=(placed,) * 4, out_specs=(placed,) * 3, check_vma=False
    )
```

```python
import functools

import jax
import jax.numpy as jnp
from jax import lax
from jax.experimental import pallas as pl
from jax.experimental.pallas import tpu as pltpu
from jax.sharding import PartitionSpec as P

MESH = pl.DeviceIdType.MESH
HEADS = 16
HEAD = 128
NY = 4
PARTS = (2, 2, 4, 4, 4)
CHUNKS = len(PARTS)
ORDER = (
    "S0", "S1", "S2", "S3", "S4", "I4", "R0", "R1", "I3", "R2", "I2", "R3",
    "T0", "T1", "I1", "R4", "Z0", "T2", "Z1", "I2", "T3", "P0", "Z2", "T4",
    "P1", "I1", "Z3", "P2", "I2", "Z4", "I1", "L0", "P3", "P4", "F0", "F1",
    "F2", "F3",
)
LIMIT = 90 << 19
START = [sum(PARTS[:c]) for c in range(CHUNKS)]
F32 = jnp.float32
BF16 = jnp.bfloat16

NN = (((1,), (0,)), ((), ()))
NT = (((1,), (1,)), ((), ()))
TN = (((0,), (0,)), ((), ()))


def dot(a, b, dims):
    return lax.dot_general(a, b, dims, preferred_element_type=F32)


def far_first(count):
    return sorted(range(1, count), key=lambda step: -min(step, count - step))


def schedule():
    order = []
    inner = 0
    for step in ORDER:
        if step[0] == "I":
            count = int(step[1:])
            order.append(("I", inner, inner + count))
            inner += count
        else:
            order.append((step[0], int(step[1:])))
    return order


def kernel(no, nz, *refs):
    refs = iter(refs)

    def take(count):
        return [next(refs) for _ in range(count)]

    q_hbm, k_hbm, v_hbm, g_hbm = take(4)
    oq, ok, ov, lq, lk, lv, ls, lw, lx, last_states = take(10)
    q, k, v, g, sg, pq, pk, pv = take(8)
    ysend, yrecv, zsend, zrecv, tsend, trecv, bsend, brecv, psend = (take(CHUNKS) for _ in range(9))
    precv = take(CHUNKS - 1)
    in_sem, send_sem, recv_sem = take(3)
    precv.append(last_states)
    length = q.shape[0]
    o = lax.axis_index("outer")
    i = lax.axis_index("inner")
    z = i // NY
    y = i % NY

    ypeers = [lax.rem(y + d, NY) for d in far_first(NY)]
    zpeers = [lax.rem(z + d, nz) for d in far_first(nz)]
    opeers = [lax.rem(o + d, no) for d in far_first(no)]

    def loads(c):
        cols = pl.ds(START[c] * HEAD, PARTS[c] * HEAD)
        return [
            pltpu.make_async_copy(src.at[:, cols], dst.at[:, cols], in_sem.at[c, j])
            for j, (src, dst) in enumerate(((k_hbm, k), (v_hbm, v), (g_hbm, g), (q_hbm, q)))
        ]

    for copy in loads(0):
        copy.start()

    barrier = pltpu.get_barrier_semaphore()
    everyone = (
        [(o, p * NY + y) for p in zpeers]
        + [(p, i) for p in opeers]
        + [(o, z * NY + p) for p in ypeers]
    )
    for peer in everyone:
        pl.semaphore_signal(barrier, inc=1, device_id=peer, device_id_type=MESH)
    for c in range(1, CHUNKS):
        for copy in loads(c):
            copy.start()

    offset = (o * (nz * NY) + i) * length
    rows = lax.broadcasted_iota(jnp.int32, (length, HEAD), 0) + offset
    scales = lax.rsqrt(rows.astype(F32) + 1.0)

    def send(src, dst, stage, c, peer):
        pltpu.make_async_remote_copy(
            src_ref=src, dst_ref=dst, send_sem=send_sem.at[stage, c], recv_sem=recv_sem.at[stage, c],
            device_id=peer, device_id_type=MESH,
        ).start()

    def arrived(ref, stage, c):
        pltpu.make_async_copy(ref, ref, recv_sem.at[stage, c]).wait()

    def states(c):
        for copy in loads(c):
            copy.wait()
        part = yrecv[c].shape[2]
        for j in range(PARTS[c]):
            cols = pl.ds((START[c] + j) * HEAD, HEAD)
            scaled = (g[:, cols].astype(F32) * scales).astype(BF16)
            sg[:, cols] = scaled
            both = (dot(k[:, cols], v[:, cols], TN), dot(q[:, cols], scaled, TN))
            for kind in range(2):
                for r in range(0, HEAD, part):
                    ysend[c][(j * HEAD + r) // part, kind] = both[kind][r:r + part].astype(BF16)
        if c == 0:
            pl.semaphore_wait(barrier, len(everyone))
        for p in ypeers:
            send(ysend[c].at[p], yrecv[c].at[y], 0, c, (o, z * NY + p))
        yrecv[c][y] = ysend[c][y]

    def group_sums(c):
        arrived(yrecv[c].at[pl.ds(0, NY - 1)], 0, c)
        total = yrecv[c][0].astype(F32)
        for p in range(1, NY):
            total = total + yrecv[c][p].astype(F32)
        sub = total.shape[1] // nz
        for p in range(nz):
            cut = slice(p * sub, (p + 1) * sub)
            zsend[c][p] = jnp.concatenate([total[0, cut], total[1, cut]], axis=0).astype(BF16)
        for p in zpeers:
            send(zsend[c].at[p], zrecv[c].at[z], 1, c, (o, p * NY + y))
        zrecv[c][z] = zsend[c][z]

    def outer_totals(c):
        arrived(zrecv[c].at[pl.ds(0, nz - 1)], 1, c)
        total = zrecv[c][0].astype(F32)
        for p in range(1, nz):
            total = total + zrecv[c][p].astype(F32)
        sub = total.shape[0] // 2
        tsend[c][0] = total[:sub]
        tsend[c][1] = total[sub:]
        for p in opeers:
            kind = jnp.where(p > o, 0, 1)
            send(tsend[c].at[kind], trecv[c].at[o], 2, c, (p, i))
        trecv[c][o] = jnp.zeros((sub, HEAD), F32)

    def offsets(c):
        arrived(trecv[c].at[pl.ds(0, no - 1)], 2, c)
        sub = trecv[c].shape[1]
        before = jnp.zeros((sub, HEAD), F32)
        after = jnp.zeros((sub, HEAD), F32)
        for p in range(no):
            part = trecv[c][p]
            before = before + jnp.where(p < o, part, 0.0)
            after = after + jnp.where(p > o, part, 0.0)
        own = [zrecv[c][p].astype(F32) for p in range(nz)]
        befores, afters = [], []
        for p in range(nz):
            befores.append(before)
            before = before + own[p][:sub]
        for p in reversed(range(nz)):
            afters.append(after)
            after = after + own[p][sub:]
        for p in range(nz):
            bsend[c][p] = jnp.concatenate([befores[p], afters[nz - 1 - p]], axis=0).astype(BF16)
        for p in zpeers:
            send(bsend[c].at[p], brecv[c].at[z], 3, c, (o, p * NY + y))
        brecv[c][z] = bsend[c][z]

    def block_states(c):
        arrived(brecv[c].at[pl.ds(0, nz - 1)], 3, c)
        sub = brecv[c].shape[1] // 2
        pieces = [brecv[c][p].astype(F32) for p in range(nz)]
        before = jnp.concatenate([piece[:sub] for piece in pieces], axis=0)
        after = jnp.concatenate([piece[sub:] for piece in pieces], axis=0)
        for r in range(NY):
            psend[c][r, 0] = before.astype(BF16)
            before = before + yrecv[c][r, 0].astype(F32)
        for r in reversed(range(NY)):
            psend[c][r, 1] = after.astype(BF16)
            after = after + yrecv[c][r, 1].astype(F32)
        for p in ypeers:
            send(psend[c].at[p], precv[c].at[y], 4, c, (o, z * NY + p))
        precv[c][y] = psend[c][y]

    def finish(c):
        arrived(precv[c].at[pl.ds(0, NY - 1)], 4, c)
        part = precv[c].shape[2]
        span = HEAD // part
        for j in range(PARTS[c]):
            cols = pl.ds((START[c] + j) * HEAD, HEAD)
            prefix, suffix = (
                jnp.concatenate([precv[c][j * span + r, kind] for r in range(span)], axis=0)
                for kind in range(2)
            )
            oq[:, cols] = (pq[:, cols] + dot(sg[:, cols], prefix, NT)).astype(BF16)
            ok[:, cols] = (pk[:, cols] + dot(v[:, cols], suffix, NT)).astype(BF16)
            ov[:, cols] = (pv[:, cols] + dot(k[:, cols], suffix, NN)).astype(BF16)

    def leave():
        cols = pl.ds(START[-1] * HEAD, PARTS[-1] * HEAD)
        for dst, src in ((lq, pq), (lk, pk), (lv, pv), (ls, sg), (lw, v), (lx, k)):
            dst[...] = src[:, cols]

    cut = length - HEAD

    def inside(head, carry):
        cols = pl.ds(pl.multiple_of(head * HEAD, HEAD), HEAD)
        kh, vh, qh, sh = k[:, cols], v[:, cols], q[:, cols], sg[:, cols]
        first = lax.broadcasted_iota(jnp.int32, (length, cut), 0)
        second = lax.broadcasted_iota(jnp.int32, (length, cut), 1)
        lower = second <= first
        upper = first <= second + HEAD
        row = lax.broadcasted_iota(jnp.int32, (HEAD, HEAD), 0)
        col = lax.broadcasted_iota(jnp.int32, (HEAD, HEAD), 1)

        def masked(a, b, mask):
            return jnp.where(mask, dot(a, b, NT), 0.0).astype(BF16)

        main = dot(masked(sh, vh[:cut], lower), kh[:cut], NN)
        rest = dot(masked(sh[cut:], vh[cut:], col <= row), kh[cut:], NN)
        pq[:cut, cols] = main[:cut]
        pq[cut:, cols] = main[cut:] + rest
        main = dot(masked(vh, sh[HEAD:], upper), qh[HEAD:], NN)
        rest = dot(masked(vh[:HEAD], sh[:HEAD], row <= col), qh[:HEAD], NN)
        pk[:HEAD, cols] = main[:HEAD] + rest
        pk[HEAD:, cols] = main[HEAD:]
        main = dot(masked(kh, qh[HEAD:], upper), sh[HEAD:], NN)
        rest = dot(masked(kh[:HEAD], qh[:HEAD], row <= col), sh[:HEAD], NN)
        pv[:HEAD, cols] = main[:HEAD] + rest
        pv[HEAD:, cols] = main[HEAD:]
        return carry

    actions = {
        "S": states, "R": group_sums, "T": outer_totals, "Z": offsets, "P": block_states, "F": finish,
    }
    for step in schedule():
        if step[0] == "I":
            lax.fori_loop(step[1], step[2], inside, 0)
        elif step[0] == "L":
            leave()
        else:
            actions[step[0]](step[1])

    arrived(last_states.at[pl.ds(0, NY - 1)], 4, CHUNKS - 1)
    for c in range(CHUNKS):
        for stage, (ref, count) in enumerate(
            ((ysend, NY), (zsend, nz), (trecv, no), (bsend, nz), (psend, NY))
        ):
            done = ref[c].at[pl.ds(0, count - 1)]
            pltpu.make_async_copy(done, done, send_sem.at[stage, c]).wait()


def outputs(oq, ok, ov, lq, lk, lv, ls, lw, lx, states, oq_hbm, ok_hbm, ov_hbm, fq, fk, fv, sem):
    early = pl.ds(0, START[-1] * HEAD)
    late = pl.ds(START[-1] * HEAD, PARTS[-1] * HEAD)
    copies = [
        pltpu.make_async_copy(src.at[:, early], dst.at[:, early], sem.at[0, j])
        for j, (src, dst) in enumerate(((oq, oq_hbm), (ok, ok_hbm), (ov, ov_hbm)))
    ]
    for copy in copies:
        copy.start()
    span = HEAD // states.shape[2]
    sides = [[], []]
    for j in range(PARTS[-1]):
        for kind in range(2):
            sides[kind].append(jnp.concatenate([states[j * span + r, kind] for r in range(span)], axis=0))
    plan = (
        (fq, lq, ls, sides[0], NT, oq_hbm), (fk, lk, lw, sides[1], NT, ok_hbm), (fv, lv, lx, sides[1], NN, ov_hbm)
    )
    for place, (full, part, left, side, dims, out) in enumerate(plan):
        for j in range(PARTS[-1]):
            cols = pl.ds(j * HEAD, HEAD)
            full[:, cols] = (part[:, cols] + dot(left[:, cols], side[j], dims)).astype(BF16)
        copy = pltpu.make_async_copy(full, out.at[:, late], sem.at[1, place])
        copy.start()
        copies.append(copy)
    for copy in copies:
        copy.wait()


def solution(mesh):
    no = mesh.shape["outer"]
    nz = mesh.shape["inner"] // NY

    def local(query_rows, key_rows, value_rows, grad_output):
        shape = query_rows.shape
        out = jax.ShapeDtypeStruct(shape, BF16)
        anywhere = pl.BlockSpec(memory_space=pltpu.HBM)
        inside = pl.BlockSpec(memory_space=pltpu.VMEM)
        rows = [heads * HEAD // NY for heads in PARTS]

        def buffers(make):
            return [make(count) for count in rows]

        wide = buffers(lambda count: pltpu.VMEM((NY, 2, count, HEAD), BF16))
        thin = buffers(lambda count: pltpu.VMEM((nz, 2 * (count // nz), HEAD), BF16))
        length, tail = shape[0], PARTS[-1] * HEAD
        narrow = jax.ShapeDtypeStruct((length, tail), BF16)
        sums = jax.ShapeDtypeStruct((length, tail), F32)
        last = jax.ShapeDtypeStruct((NY, 2, rows[-1], HEAD), BF16)
        held = pl.pallas_call(
            functools.partial(kernel, no, nz),
            name="linear_attention_grads",
            out_shape=(out,) * 3 + (sums,) * 3 + (narrow,) * 3 + (last,),
            in_specs=[anywhere] * 4,
            out_specs=(inside,) * 10,
            scratch_shapes=(
                [pltpu.VMEM(shape, BF16)] * 5
                + [pltpu.VMEM(shape, F32)] * 3
                + wide * 2
                + thin * 2
                + buffers(lambda count: pltpu.VMEM((2, count // nz, HEAD), F32))
                + buffers(lambda count: pltpu.VMEM((no, count // nz, HEAD), F32))
                + thin * 2
                + wide
                + wide[:-1]
                + [
                    pltpu.SemaphoreType.DMA((CHUNKS, 4)),
                    pltpu.SemaphoreType.DMA((5, CHUNKS)),
                    pltpu.SemaphoreType.DMA((5, CHUNKS)),
                ]
            ),
            compiler_params=pltpu.CompilerParams(
                collective_id=0, has_side_effects=True, vmem_limit_bytes=LIMIT
            ),
        )(query_rows, key_rows, value_rows, grad_output)
        return pl.pallas_call(
            outputs,
            name="write_grads",
            out_shape=(out, out, out),
            in_specs=[inside] * 10,
            out_specs=(anywhere,) * 3,
            scratch_shapes=[pltpu.VMEM((length, tail), BF16)] * 3 + [pltpu.SemaphoreType.DMA((2, 3))],
            compiler_params=pltpu.CompilerParams(vmem_limit_bytes=8 << 20),
        )(*held)

    placed = P(("outer", "inner"), None)
    return jax.shard_map(
        local, mesh=mesh, in_specs=(placed,) * 4, out_specs=(placed,) * 3, check_vma=False
    )
```
